256 devices in a mesh: seq: 4 (over x), vocab: 64 (over y, z, core).
Axes of the slice: x: 4, y: 4, z: 8, core: 2. Of those that a mesh axis runs over, the one named last changes fastest.
Arguments:
- teacher_hidden: bfloat16 [1024, 8192], P(None, 'seq'), may hold values from -480 to 480
- teacher_head: bfloat16 [8192, 81920], P('seq', 'vocab'), may hold values from -1 to 1
- student_hidden: bfloat16 [1024, 3584], P(None, 'seq'), may hold values from -480 to 480
- student_head: bfloat16 [3584, 81920], P('seq', 'vocab'), may hold values from -1 to 1
- kept: int32 [8, 64], replicated, may hold values from 0 to 639, as said below
Outputs:
- loss_rows: float32 [1024], P('seq')
- hidden_grad: bfloat16 [1024, 3584], P('vocab', 'seq')
- head_grad: bfloat16 [3584, 81920], P('seq', 'vocab')
The draws below stay inside these ranges and needn't reach their ends.
Inputs may be any that keep to these rules, and one draw needn't show every extreme that they name: `kept`: each row holds 64 distinct block ids in ascending order. In every row at most 4 of them lie within one run of 10 consecutive blocks starting at a multiple of 10, and in every row some such run holds exactly 4.
All inputs are finite; a program needn't handle non-finite values.
Results may differ from the reference program's by a relative error of at most 0.0049.
Values may be sent and summed in bfloat16 or wider, within the bound.
No kernel may reach another device: no remote copies, remote signals or barrier semaphores. Data moves between devices by JAX's collectives and lax.ppermute only.
A program may use at most 128 MiB of HBM per device.

```python
import jax
import jax.numpy as jnp
from jax import lax

DT = 8192
DS = 3584
VOCAB = 81920
BLOCK = 128
KEPT = 64
TOKENS = 1024
ROW_BLOCK_TOTAL = 8
NBLOCKS = 640
NB_DEV = 10
MOSTB = 4


def head_block(head_key, number, depth):
    values = jnp.clip(jax.random.normal(jax.random.fold_in(head_key, number), (depth, BLOCK), jnp.float32), -4.0, 4.0)
    values = values * (1.0 / float(depth) ** 0.5)
    return values.astype(jnp.bfloat16).astype(jnp.float32)


def whole_head(head_key, depth):
    blocks = jax.vmap(lambda number: head_block(head_key, number, depth))(jnp.arange(NBLOCKS, dtype=jnp.int32))
    return jnp.transpose(blocks, (1, 0, 2)).reshape(depth, VOCAB)


def scaled_rows(key, depth):
    values = jnp.clip(jax.random.normal(jax.random.fold_in(key, 3), (TOKENS, depth), jnp.float32), -6.0, 6.0)
    return values


def draw_teacher_head(key, part):
    return whole_head(jax.random.fold_in(key, 31), DT).astype(jnp.bfloat16)


def draw_student_head(key, part):
    return whole_head(jax.random.fold_in(key, 37), DS).astype(jnp.bfloat16)


def draw_teacher_hidden(key, part):
    return scaled_rows(jax.random.fold_in(key, 11), DT).astype(jnp.bfloat16)


def draw_student_hidden(key, part):
    return scaled_rows(jax.random.fold_in(key, 23), DS).astype(jnp.bfloat16)


def draw_kept(key, part):
    device_shards = NBLOCKS // NB_DEV
    slot_entries = device_shards * MOSTB
    random_keys = jax.random.split(jax.random.fold_in(key, 7), 4)
    extra_boost = jax.random.randint(random_keys[0], (ROW_BLOCK_TOTAL, device_shards), 0, 3)
    forced_pick = jax.random.randint(random_keys[1], (ROW_BLOCK_TOTAL,), 0, device_shards)
    extra_boost = jnp.where(jnp.arange(device_shards)[None, :] == forced_pick[:, None], 3, extra_boost)
    random_noise = jax.random.randint(random_keys[2], (ROW_BLOCK_TOTAL, device_shards, MOSTB), 0, 1024)
    primary_choice = (extra_boost[:, :, None] * 1024 + random_noise).reshape(ROW_BLOCK_TOTAL, slot_entries)
    scores = primary_choice * slot_entries + jnp.arange(slot_entries)[None, :]
    unused, chosen = lax.top_k(scores, KEPT)
    shard_of = chosen // MOSTB
    slot_of = chosen % MOSTB
    offsets = jax.random.randint(random_keys[3], (ROW_BLOCK_TOTAL, device_shards), 0, NB_DEV)
    shift_of = jnp.take_along_axis(offsets, shard_of, axis=1)
    block_of = shard_of * NB_DEV + (shift_of + slot_of) % NB_DEV
    return jnp.sort(block_of, axis=1).astype(jnp.int32)


def setup_inputs(seed: int = 0) -> dict:
    keys = jax.random.split(jax.random.key(seed), 6)
    teacher_hidden = draw_teacher_hidden(jax.random.fold_in(keys[5], 71), 0)
    teacher_head = draw_teacher_head(jax.random.fold_in(keys[5], 71), 0)
    student_hidden = draw_student_hidden(jax.random.fold_in(keys[5], 71), 0)
    student_head = draw_student_head(jax.random.fold_in(keys[5], 71), 0)
    kept = draw_kept(jax.random.fold_in(keys[5], 71), 0)
    return dict(teacher_hidden=teacher_hidden, teacher_head=teacher_head, student_hidden=student_hidden, student_head=student_head, kept=kept)


masked_value = -1e30
loss_scale = 2048.0


def reference(teacher_hidden, teacher_head, student_hidden, student_head, kept):
    block_ids = jnp.arange(NBLOCKS, dtype=jnp.int32)

    def one_block(block_number):
        row_start = (block_number * BLOCK).astype(jnp.int32)
        teacher_rows = lax.dynamic_slice_in_dim(teacher_hidden, row_start, BLOCK, 0)
        student_rows = lax.dynamic_slice_in_dim(student_hidden, row_start, BLOCK, 0)
        teacher_logits = jnp.dot(teacher_rows, teacher_head, preferred_element_type=jnp.float32)
        student_logits = jnp.dot(student_rows, student_head, preferred_element_type=jnp.float32)
        chosen = lax.dynamic_index_in_dim(kept, block_number, 0, keepdims=False)
        block_mask = jnp.any(chosen[:, None] == block_ids[None, :], axis=0)
        column_mask = jnp.repeat(block_mask, BLOCK)[None, :]
        teacher_max = jnp.max(jnp.where(column_mask, teacher_logits, masked_value), axis=1)
        weights = jnp.where(column_mask, jnp.exp(teacher_logits - teacher_max[:, None]), 0.0)
        teacher_total = jnp.sum(weights, axis=1)
        cross_total = jnp.sum(weights * student_logits, axis=1)
        self_total = jnp.sum(weights * teacher_logits, axis=1)
        student_max = jnp.max(student_logits, axis=1)
        student_exp = jnp.exp(student_logits - student_max[:, None])
        student_total = jnp.sum(student_exp, axis=1)
        loss_rows = (self_total / teacher_total - teacher_max - jnp.log(teacher_total)) - (cross_total / teacher_total - student_max - jnp.log(student_total))
        teacher_prob = weights / teacher_total[:, None]
        student_prob = student_exp / student_total[:, None]
        grad_logits = (loss_scale * (student_prob - teacher_prob)).astype(jnp.bfloat16)
        return loss_rows, grad_logits

    loss_rows, grad_logits = lax.map(one_block, jnp.arange(ROW_BLOCK_TOTAL, dtype=jnp.int32))
    grad_logits = grad_logits.reshape(TOKENS, VOCAB)
    hidden_grad = jnp.dot(grad_logits, student_head.T, preferred_element_type=jnp.float32).astype(jnp.bfloat16)
    head_grad = jnp.dot(student_hidden.T, grad_logits, preferred_element_type=jnp.float32).astype(jnp.bfloat16)
    return loss_rows.reshape(TOKENS), hidden_grad, head_grad
```

```python
import functools

import jax
import jax.numpy as jnp
from jax import lax
from jax.experimental import pallas as pl
from jax.experimental.pallas import tpu as pltpu
from jax.sharding import Mesh
from jax.sharding import PartitionSpec as P

VOCAB = ("y", "z", "c")
BLOCK = 128
MOST = 4
GROUP = 16
ROW_BLOCKS = 8
SLOTS = ROW_BLOCKS * MOST
STATS = 5
HALF_ROWS = ROW_BLOCKS * GROUP

masked_value = -1e30
loss_scale = 2048.0
f32 = jnp.float32
bf16 = jnp.bfloat16
MIB = 1024 * 1024


def whole(shape):
    return pl.BlockSpec(shape, lambda i: (0,) * len(shape))


def call(kernel, scalars, arrays, outs, scratch=(), limit=52):
    return pl.pallas_call(
        kernel,
        grid=(1,),
        in_specs=[pl.BlockSpec(memory_space=pltpu.SMEM)] * len(scalars)
        + [whole(array.shape) for array in arrays],
        out_specs=[whole(shape) for shape, _ in outs],
        out_shape=[jax.ShapeDtypeStruct(shape, dtype) for shape, dtype in outs],
        scratch_shapes=list(scratch),
        compiler_params=pltpu.CompilerParams(vmem_limit_bytes=limit * MIB),
    )(*scalars, *arrays)


def group_rows(row_block, owner, half):
    return pl.ds(pl.multiple_of(row_block * BLOCK + owner * 32 + half * GROUP, GROUP), GROUP)


def teacher_slots(owners, ids, valid, hidden, head, lhs, store):
    def row_block(r, carry):
        for place in range(4):
            rows = pl.ds(pl.multiple_of(r * BLOCK + owners[place] * 32, 32), 32)
            lhs[place * 32 : (place + 1) * 32, :] = hidden[rows, :]
        rows = pl.ds(pl.multiple_of(r * GROUP, GROUP), GROUP)
        for m in range(MOST):
            slot = r * MOST + m

            @pl.when(valid[slot] > 0)
            def _():
                cols = pl.ds(pl.multiple_of(ids[slot] * BLOCK, BLOCK), BLOCK)
                part = jnp.dot(lhs[...], head[:, cols], preferred_element_type=f32)
                for place in range(4):
                    store(rows, m, place, part[place * 32 : (place + 1) * 32])

        return carry

    lax.fori_loop(0, ROW_BLOCKS, row_block, 0)


def gather_rows(owners, hidden, lhs):
    for half in range(2):
        for place in range(4):
            for r in range(ROW_BLOCKS):
                low = (half * 4 + place) * HALF_ROWS + r * GROUP
                lhs[low : low + GROUP, :] = hidden[group_rows(r, owners[place], half), :]


def student_kernel(owners, hidden, head, far_l, far_r, nxt0, prv0, own0, nxt1, prv1, own1, lhs):
    gather_rows(owners, hidden, lhs)
    width = far_l.shape[2]
    for half, wide in enumerate(((nxt0, prv0, own0), (nxt1, prv1, own1))):
        rows = slice(half * 4 * HALF_ROWS, (half + 1) * 4 * HALF_ROWS)
        for side, far in enumerate((far_l, far_r)):
            cols = slice(side * width, (side + 1) * width)
            part = jnp.dot(lhs[rows], head[:, cols], preferred_element_type=f32)
            far[half] = part[:HALF_ROWS]
            for place, ref in enumerate(wide):
                ref[:, cols] = part[(place + 1) * HALF_ROWS : (place + 2) * HALF_ROWS]


def student_partial(owners, hidden, head):
    cols = head.shape[1]
    return call(
        student_kernel,
        [owners],
        [hidden, head],
        [((2, HALF_ROWS, cols // 2), f32)] * 2 + [((HALF_ROWS, cols), f32)] * 6,
        [pltpu.VMEM(hidden.shape, bf16)],
    )


def teacher_kernel(owners, ids, valid, hidden, head, far_l, far_r, nxt, prv, own, lhs):
    wide = (nxt, prv, own)
    for ref in (far_l, far_r, *wide):
        ref[...] = jnp.zeros(ref.shape, f32)

    def store(rows, m, place, part):
        for half in range(2):
            value = part[half * GROUP : (half + 1) * GROUP]
            if place == 0:
                low = (m % 2) * BLOCK
                (far_l, far_r)[m // 2][half, rows, low : low + BLOCK] = value
            else:
                wide[place - 1][half, rows, m * BLOCK : (m + 1) * BLOCK] = value

    teacher_slots(owners, ids, valid, hidden, head, lhs, store)


def teacher_partial(owners, ids, valid, hidden, head):
    return call(
        teacher_kernel,
        [owners, ids, valid],
        [hidden, head],
        [((2, HALF_ROWS, 2 * BLOCK), f32)] * 2 + [((2, HALF_ROWS, MOST * BLOCK), f32)] * 3,
        [pltpu.VMEM((BLOCK, head.shape[0]), bf16)],
    )


def student_merge_kernel(half, nxt, prv, from_prev, from_next, to_next, to_prev):
    cut = from_prev.shape[2]
    to_next[:, :cut] = nxt[:, :cut] + from_prev[half]
    to_next[:, cut:] = nxt[:, cut:]
    to_prev[:, :cut] = prv[:, :cut]
    to_prev[:, cut:] = prv[:, cut:] + from_next[half]


def teacher_merge_kernel(nxt, prv, from_prev, from_next, to_next, to_prev):
    cut = from_prev.shape[2]
    to_next[:, :, :cut] = nxt[:, :, :cut] + from_prev[...]
    to_next[:, :, cut:] = nxt[:, :, cut:]
    to_prev[:, :, :cut] = prv[:, :, :cut]
    to_prev[:, :, cut:] = prv[:, :, cut:] + from_next[...]


def merge(kernel, *parts):
    return call(kernel, [], parts, [(parts[0].shape, f32)] * 2)


def turn_kernel(owners, core, hidden, head, turned_hidden, turned_head, lhs):
    gather_rows(owners, hidden, lhs)
    turned_hidden[...] = lhs[...].T
    for part in range(2):
        rows = pl.ds(pl.multiple_of(core[part] * 384, 128), 512)
        turned_head[part] = head[rows, :].T


def turned(owners, core, hidden, head):
    return call(
        turn_kernel,
        [owners, core],
        [hidden, head],
        [((hidden.shape[1], hidden.shape[0]), bf16), ((2, head.shape[1], 512), bf16)],
        [pltpu.VMEM(hidden.shape, bf16)],
    )


def stats_kernel(half, ids, valid, own, from_prev, from_next, town, tprev, tnext, first, e_out, w_out, stats, logits, tile):
    lane = lax.broadcasted_iota(jnp.int32, (GROUP, BLOCK), 1)
    for r in range(ROW_BLOCKS):
        rows = slice(r * GROUP, (r + 1) * GROUP)
        student = own[rows] + from_prev[rows] + from_next[rows]
        logits[rows] = student
        student_top = jnp.max(student, axis=1, keepdims=True)
        student_exp = jnp.exp(student - student_top)
        e_out[rows] = student_exp
        student_total = jnp.sum(student_exp, axis=1, keepdims=True)
        teacher = []
        for m in range(MOST):
            cols = slice(m * BLOCK, (m + 1) * BLOCK)
            value = town[half, rows, cols] + tprev[half, rows, cols] + tnext[half, rows, cols]
            teacher.append(jnp.where(valid[r * MOST + m] > 0, value, masked_value))
        highest = functools.reduce(jnp.maximum, teacher)
        teacher_top = jnp.max(highest, axis=1, keepdims=True)
        total = gap = jnp.zeros((GROUP, BLOCK), f32)
        for m in range(MOST):
            slot = r * MOST + m
            weight = jnp.where(valid[slot] > 0, jnp.exp(teacher[m] - teacher_top), 0.0)
            w_out[slot] = weight
            cols = pl.ds(pl.multiple_of(ids[slot] * BLOCK, BLOCK), BLOCK)
            total += weight
            gap += weight * (teacher[m] - logits[rows, cols])
        columns = (
            teacher_top,
            jnp.sum(total, axis=1, keepdims=True),
            jnp.sum(gap, axis=1, keepdims=True),
            student_top,
            student_total,
        )
        line = jnp.zeros((GROUP, BLOCK), f32)
        for k, column in enumerate(columns):
            line = jnp.where(lane == k, column, line)
        tile[rows] = line
    if half == 0:
        stats[...] = tile[...].T[:8]
    else:
        both = (first[...], tile[...].T[:8])
        lines = [jnp.concatenate([part[k : k + 1] for k in range(STATS)], axis=1) for part in both]
        stats[...] = jnp.broadcast_to(jnp.concatenate(lines, axis=0)[None], stats.shape)


def local_stats(half, ids, valid, student, teacher, first, sent):
    cols = student[0].shape[1]
    return call(
        functools.partial(stats_kernel, half),
        [ids, valid],
        [*student, *teacher, first],
        [((HALF_ROWS, cols), f32), ((SLOTS, GROUP, BLOCK), f32), (sent, f32)],
        [pltpu.VMEM((HALF_ROWS, cols), f32), pltpu.VMEM((HALF_ROWS, BLOCK), f32)],
    )


def grad_kernel(half, ids, e_in, w_in, mine, merged, grad, loss, work):
    def stat(k):
        return merged[:, half, k * BLOCK : (k + 1) * BLOCK]

    def own_stat(k):
        return mine[0, half : half + 1, k * BLOCK : (k + 1) * BLOCK]

    teacher_top = jnp.max(stat(0), axis=0, keepdims=True)
    teacher_scale = jnp.exp(stat(0) - teacher_top)
    teacher_total = jnp.sum(stat(1) * teacher_scale, axis=0, keepdims=True)
    gap = jnp.sum(stat(2) * teacher_scale, axis=0, keepdims=True)
    student_top = jnp.max(stat(3), axis=0, keepdims=True)
    student_total = jnp.sum(stat(4) * jnp.exp(stat(3) - student_top), axis=0, keepdims=True)
    loss_row = (gap / teacher_total - teacher_top - jnp.log(teacher_total)) + (
        student_top + jnp.log(student_total)
    )
    loss[...] = jnp.broadcast_to(loss_row, loss.shape)
    student_factor = loss_scale * jnp.exp(own_stat(3) - student_top) / student_total
    teacher_factor = loss_scale * jnp.exp(own_stat(0) - teacher_top) / teacher_total
    line = lax.broadcasted_iota(jnp.int32, (HALF_ROWS, BLOCK), 0)
    factors = jnp.where(line == 0, student_factor, jnp.where(line == 1, teacher_factor, 0.0)).T
    work[...] = e_in[...] * factors[:, 0:1]
    for r in range(ROW_BLOCKS):
        rows = slice(r * GROUP, (r + 1) * GROUP)
        factor = factors[rows, 1:2]
        for m in range(MOST):
            slot = r * MOST + m
            cols = pl.ds(pl.multiple_of(ids[slot] * BLOCK, BLOCK), BLOCK)
            work[rows, cols] = work[rows, cols] - factor * w_in[slot]
    grad[...] = work[...].astype(bf16)


def logit_grads(half, ids, e_in, w_in, mine, merged):
    return call(
        functools.partial(grad_kernel, half),
        [ids],
        [e_in, w_in, mine, merged],
        [(e_in.shape, bf16), ((8, BLOCK), f32)],
        [pltpu.VMEM(e_in.shape, f32)],
    )


def hidden_kernel(owners, far, after, before, own, turned_head, keep, give, rows, work):
    for place, piece in enumerate((far, after, before, own)):
        rows[place * HALF_ROWS : (place + 1) * HALF_ROWS, :] = piece[...]
    for part, out in ((1, give), (0, keep)):
        work[...] = jnp.dot(rows[...], turned_head[part], preferred_element_type=f32)
        for place in range(4):
            zl = owners[place]
            for y in range(4):
                for zh in range(2):
                    low = place * HALF_ROWS + y * 32 + zh * GROUP
                    out[y, zh * 4 + zl] = work[low : low + GROUP, :]


def hidden_partial(owners, pieces, turned_head):
    width = turned_head.shape[2]
    return call(
        hidden_kernel,
        [owners],
        [*pieces, turned_head],
        [((4, 8, GROUP, width), f32)] * 2,
        [pltpu.VMEM((4 * HALF_ROWS, pieces[0].shape[1]), bf16), pltpu.VMEM((4 * HALF_ROWS, width), f32)],
    )


def head_kernel(turned_hidden, *refs):
    pieces = refs[:8]
    out, grads = refs[8:]
    for k in range(8):
        grads[k * HALF_ROWS : (k + 1) * HALF_ROWS, :] = pieces[k][...]
    step = 256
    for low in range(0, out.shape[1], step):
        cols = slice(low, low + step)
        out[:, cols] = jnp.dot(turned_hidden[...], grads[:, cols], preferred_element_type=f32).astype(bf16)


def head_total(turned_hidden, pieces):
    depth, tokens = turned_hidden.shape
    cols = pieces[0].shape[1]
    return call(
        head_kernel,
        [],
        [turned_hidden, *pieces],
        [((depth, cols), bf16)],
        [pltpu.VMEM((tokens, cols), bf16)],
    )[0]


def after(earlier, arrays):
    return lax.optimization_barrier((earlier, arrays))[1]


def shift(array, axis, step):
    size = lax.axis_size(axis)
    return lax.ppermute(array, axis, [(k, (k + step) % size) for k in range(size)])


def slots_of(kept, first, blocks):
    before = jnp.sum((kept < first).astype(jnp.int32), axis=1)
    place = jnp.arange(kept.shape[1], dtype=jnp.int32)
    wanted = before[:, None] + jnp.arange(MOST, dtype=jnp.int32)[None, :]
    chosen = (place[None, None, :] == wanted[:, :, None]) & (kept < first + blocks)[:, None, :]
    ids = jnp.sum(jnp.where(chosen, kept[:, None, :] - first, 0), axis=2)
    valid = jnp.any(chosen, axis=2)
    return ids.reshape(-1), valid.astype(jnp.int32).reshape(-1)


def body(teacher_hidden, teacher_head, student_hidden, student_head, kept):
    blocks = teacher_head.shape[1] // BLOCK
    x, c = lax.axis_index("x"), lax.axis_index("c")
    around = jnp.array([2, 1, 3, 0], jnp.int32)
    owners = ((x + around) % 4).astype(jnp.int32)
    core = jnp.stack([c, 1 - c]).astype(jnp.int32)
    ids, valid = slots_of(kept, lax.axis_index(VOCAB) * blocks, blocks)

    def to_both(to_next, to_prev):
        return shift(to_next, "x", 1), shift(to_prev, "x", -1)

    far_l, far_r, nxt0, prv0, own0, nxt1, prv1, own1 = student_partial(
        owners, student_hidden, student_head
    )
    tfar_l, tfar_r, tnxt, tprv, town = teacher_partial(
        owners, ids, valid, *after(own1, (teacher_hidden, teacher_head))
    )
    far, tfar = to_both(far_l, far_r), to_both(tfar_l, tfar_r)
    merged0 = merge(functools.partial(student_merge_kernel, 0), *after(town, (nxt0, prv0)), *far)
    tmerged = merge(teacher_merge_kernel, *after(merged0[0], (tnxt, tprv)), *tfar)
    merged1 = merge(
        functools.partial(student_merge_kernel, 1), *after(tmerged[0], (nxt1, prv1)), *far
    )
    logits0 = (own0, *to_both(*merged0))
    teacher = (town, *to_both(*tmerged))
    logits1 = (own1, *to_both(*merged1))
    turned_hidden, turned_head = turned(owners, core, *after(merged1[0], (student_hidden, student_head)))

    def spread(grad):
        return shift(grad, "x", 2), shift(grad, "x", -1), shift(grad, "x", 1), grad

    def row_sums(pieces):
        keep, give = hidden_partial(owners, pieces, turned_head)
        return keep, shift(give, "c", 1)

    devices = lax.axis_size(VOCAB)
    nothing = jnp.zeros((8, BLOCK), f32)
    e0, w0, first = local_stats(
        0, ids, valid, after(turned_head, logits0), teacher, nothing, (8, BLOCK)
    )
    e1, w1, mine = local_stats(1, ids, valid, logits1, teacher, first, (devices, 2, STATS * BLOCK))
    every = lax.all_to_all(mine, VOCAB, 0, 0, tiled=True)
    grad0, loss0 = logit_grads(0, ids, e0, w0, mine, every)
    grad1, loss1 = logit_grads(1, ids, e1, w1, mine, after(grad0, every))
    pieces0, pieces1 = after(grad1, spread(grad0)), spread(grad1)
    keep0, got0 = row_sums(pieces0)
    over_y0 = lax.all_to_all(keep0 + got0, "y", 0, 0, tiled=True)
    rows0 = over_y0.sum(axis=0)
    pieces1 = after(rows0, pieces1)
    keep1, got1 = row_sums(pieces1)
    over_y1 = lax.all_to_all(keep1 + got1, "y", 0, 0, tiled=True)
    loss = jnp.concatenate([loss0, loss1], axis=1)
    losses = [loss] + [shift(loss, "x", step) for step in (1, 2, 3)]
    head_grad = head_total(turned_hidden, (*pieces0, *pieces1))
    (head_grad, losses), over_y1 = lax.optimization_barrier(((head_grad, losses), over_y1))
    both = jnp.concatenate([rows0, over_y1.sum(axis=0)], axis=1)
    both = lax.all_to_all(both, "z", 0, 0, tiled=True)
    both = both.sum(axis=0).astype(bf16)
    sum0, sum1 = both[:GROUP], both[GROUP:]
    keep = jnp.where(c == 0, sum0, sum1)
    got = shift(jnp.where(c == 0, sum1, sum0), "c", 1)
    low, high = jnp.where(c == 0, keep, got), jnp.where(c == 0, got, keep)
    hidden_grad = jnp.concatenate([low, high[:, BLOCK:]], axis=1)

    row = jnp.stack([part[0] for part in losses]).reshape(4, 2, 4, 2, GROUP)
    row = lax.dynamic_index_in_dim(row, x, 2, keepdims=False)
    row = jnp.take(row, (x - jnp.arange(4)) % 4, axis=0)
    loss_rows = row.transpose(2, 0, 1, 3).reshape(-1)
    return loss_rows, hidden_grad, head_grad


def solution(mesh):
    split = Mesh(mesh.devices.reshape(4, 4, 8, 2), ("x", "y", "z", "c"))
    in_specs = (P(None, "x"), P("x", VOCAB), P(None, "x"), P("x", VOCAB), P())
    out_specs = (P("x"), P(VOCAB, "x"), P("x", VOCAB))
    return jax.shard_map(body, mesh=split, in_specs=in_specs, out_specs=out_specs, check_vma=False)
```

```python
import functools

import jax
import jax.numpy as jnp
from jax import lax
from jax.experimental import pallas as pl
from jax.experimental.pallas import tpu as pltpu
from jax.sharding import Mesh
from jax.sharding import PartitionSpec as P

VOCAB = ("y", "z", "c")
BLOCK = 128
MOST = 4
GROUP = 16
ROW_BLOCKS = 8
SLOTS = ROW_BLOCKS * MOST
STATS = 5
HALF_ROWS = ROW_BLOCKS * GROUP

masked_value = -1e30
loss_scale = 2048.0
f32 = jnp.float32
bf16 = jnp.bfloat16
MIB = 1024 * 1024


def whole(shape):
    return pl.BlockSpec(shape, lambda i: (0,) * len(shape))


def call(kernel, scalars, arrays, outs, scratch=(), limit=52):
    return pl.pallas_call(
        kernel,
        grid=(1,),
        in_specs=[pl.BlockSpec(memory_space=pltpu.SMEM)] * len(scalars)
        + [whole(array.shape) for array in arrays],
        out_specs=[whole(shape) for shape, _ in outs],
        out_shape=[jax.ShapeDtypeStruct(shape, dtype) for shape, dtype in outs],
        scratch_shapes=list(scratch),
        compiler_params=pltpu.CompilerParams(vmem_limit_bytes=limit * MIB),
    )(*scalars, *arrays)


def group_rows(row_block, owner, half):
    return pl.ds(pl.multiple_of(row_block * BLOCK + owner * 32 + half * GROUP, GROUP), GROUP)


def teacher_slots(owners, ids, valid, hidden, head, lhs, store):
    def row_block(r, carry):
        for place in range(4):
            rows = pl.ds(pl.multiple_of(r * BLOCK + owners[place] * 32, 32), 32)
            lhs[place * 32 : (place + 1) * 32, :] = hidden[rows, :]
        rows = pl.ds(pl.multiple_of(r * GROUP, GROUP), GROUP)
        for m in range(MOST):
            slot = r * MOST + m

            @pl.when(valid[slot] > 0)
            def _():
                cols = pl.ds(pl.multiple_of(ids[slot] * BLOCK, BLOCK), BLOCK)
                part = jnp.dot(lhs[...], head[:, cols], preferred_element_type=f32)
                for place in range(4):
                    store(rows, m, place, part[place * 32 : (place + 1) * 32])

        return carry

    lax.fori_loop(0, ROW_BLOCKS, row_block, 0)


def gather_rows(owners, hidden, lhs, places=range(4)):
    low = 0
    for half in range(2):
        for place in places:
            for r in range(ROW_BLOCKS):
                lhs[low : low + GROUP, :] = hidden[group_rows(r, owners[place], half), :]
                low += GROUP


def student_far_kernel(owners, hidden, head, far_l, far_r, lhs):
    gather_rows(owners, hidden, lhs, (0,))
    width = far_l.shape[2]
    for side, far in enumerate((far_l, far_r)):
        cols = slice(side * width, (side + 1) * width)
        part = jnp.dot(lhs[...], head[:, cols], preferred_element_type=f32)
        far[0] = part[:HALF_ROWS]
        far[1] = part[HALF_ROWS:]


def student_far(owners, hidden, head):
    tokens, depth = hidden.shape
    return call(
        student_far_kernel,
        [owners],
        [hidden, head],
        [((2, HALF_ROWS, head.shape[1] // 2), f32)] * 2,
        [pltpu.VMEM((tokens // 4, depth), bf16)],
    )


def student_near_kernel(owners, hidden, head, nxt0, prv0, own0, nxt1, prv1, own1, lhs):
    gather_rows(owners, hidden, lhs, (1, 2, 3))
    width = head.shape[1] // 2
    for half, wide in enumerate(((nxt0, prv0, own0), (nxt1, prv1, own1))):
        rows = slice(half * 3 * HALF_ROWS, (half + 1) * 3 * HALF_ROWS)
        for side in range(2):
            cols = slice(side * width, (side + 1) * width)
            part = jnp.dot(lhs[rows], head[:, cols], preferred_element_type=f32)
            for place, ref in enumerate(wide):
                ref[:, cols] = part[place * HALF_ROWS : (place + 1) * HALF_ROWS]


def student_near(owners, hidden, head):
    tokens, depth = hidden.shape
    return call(
        student_near_kernel,
        [owners],
        [hidden, head],
        [((HALF_ROWS, head.shape[1]), f32)] * 6,
        [pltpu.VMEM((tokens // 4 * 3, depth), bf16)],
    )


def teacher_kernel(owners, ids, valid, hidden, head, far_l, far_r, nxt, prv, own, lhs):
    wide = (nxt, prv, own)
    for ref in (far_l, far_r, *wide):
        ref[...] = jnp.zeros(ref.shape, f32)

    def store(rows, m, place, part):
        for half in range(2):
            value = part[half * GROUP : (half + 1) * GROUP]
            if place == 0:
                low = (m % 2) * BLOCK
                (far_l, far_r)[m // 2][half, rows, low : low + BLOCK] = value
            else:
                wide[place - 1][half, rows, m * BLOCK : (m + 1) * BLOCK] = value

    teacher_slots(owners, ids, valid, hidden, head, lhs, store)


def teacher_partial(owners, ids, valid, hidden, head):
    return call(
        teacher_kernel,
        [owners, ids, valid],
        [hidden, head],
        [((2, HALF_ROWS, 2 * BLOCK), f32)] * 2 + [((2, HALF_ROWS, MOST * BLOCK), f32)] * 3,
        [pltpu.VMEM((BLOCK, head.shape[0]), bf16)],
    )


def student_merge_kernel(half, nxt, prv, from_prev, from_next, to_next, to_prev):
    cut = from_prev.shape[2]
    to_next[:, :cut] = nxt[:, :cut] + from_prev[half]
    to_next[:, cut:] = nxt[:, cut:]
    to_prev[:, :cut] = prv[:, :cut]
    to_prev[:, cut:] = prv[:, cut:] + from_next[half]


def teacher_merge_kernel(nxt, prv, from_prev, from_next, to_next, to_prev):
    cut = from_prev.shape[2]
    to_next[:, :, :cut] = nxt[:, :, :cut] + from_prev[...]
    to_next[:, :, cut:] = nxt[:, :, cut:]
    to_prev[:, :, :cut] = prv[:, :, :cut]
    to_prev[:, :, cut:] = prv[:, :, cut:] + from_next[...]


def merge(kernel, *parts):
    return call(kernel, [], parts, [(parts[0].shape, f32)] * 2)


def turn_kernel(owners, core, hidden, head, turned_hidden, turned_head, lhs):
    gather_rows(owners, hidden, lhs)
    turned_hidden[...] = lhs[...].T
    for part in range(2):
        rows = pl.ds(pl.multiple_of(core[part] * 384, 128), 512)
        turned_head[part] = head[rows, :].T


def turned(owners, core, hidden, head):
    return call(
        turn_kernel,
        [owners, core],
        [hidden, head],
        [((hidden.shape[1], hidden.shape[0]), bf16), ((2, head.shape[1], 512), bf16)],
        [pltpu.VMEM(hidden.shape, bf16)],
    )


def stats_kernel(half, ids, valid, own, from_prev, from_next, town, tprev, tnext, first, e_out, w_out, stats, logits, tile):
    lane = lax.broadcasted_iota(jnp.int32, (GROUP, BLOCK), 1)
    for r in range(ROW_BLOCKS):
        rows = slice(r * GROUP, (r + 1) * GROUP)
        student = own[rows] + from_prev[rows] + from_next[rows]
        logits[rows] = student
        student_top = jnp.max(student, axis=1, keepdims=True)
        student_exp = jnp.exp(student - student_top)
        e_out[rows] = student_exp
        student_total = jnp.sum(student_exp, axis=1, keepdims=True)
        teacher = []
        for m in range(MOST):
            cols = slice(m * BLOCK, (m + 1) * BLOCK)
            value = town[half, rows, cols] + tprev[half, rows, cols] + tnext[half, rows, cols]
            teacher.append(jnp.where(valid[r * MOST + m] > 0, value, masked_value))
        highest = functools.reduce(jnp.maximum, teacher)
        teacher_top = jnp.max(highest, axis=1, keepdims=True)
        total = gap = jnp.zeros((GROUP, BLOCK), f32)
        for m in range(MOST):
            slot = r * MOST + m
            weight = jnp.where(valid[slot] > 0, jnp.exp(teacher[m] - teacher_top), 0.0)
            w_out[slot] = weight
            cols = pl.ds(pl.multiple_of(ids[slot] * BLOCK, BLOCK), BLOCK)
            total += weight
            gap += weight * (teacher[m] - logits[rows, cols])
        columns = (
            teacher_top,
            jnp.sum(total, axis=1, keepdims=True),
            jnp.sum(gap, axis=1, keepdims=True),
            student_top,
            student_total,
        )
        line = jnp.zeros((GROUP, BLOCK), f32)
        for k, column in enumerate(columns):
            line = jnp.where(lane == k, column, line)
        tile[rows] = line
    if half == 0:
        stats[...] = tile[...].T[:8]
    else:
        both = (first[...], tile[...].T[:8])
        lines = [jnp.concatenate([part[k : k + 1] for k in range(STATS)], axis=1) for part in both]
        stats[...] = jnp.broadcast_to(jnp.concatenate(lines, axis=0)[None], stats.shape)


def local_stats(half, ids, valid, student, teacher, first, sent):
    cols = student[0].shape[1]
    return call(
        functools.partial(stats_kernel, half),
        [ids, valid],
        [*student, *teacher, first],
        [((HALF_ROWS, cols), f32), ((SLOTS, GROUP, BLOCK), f32), (sent, f32)],
        [pltpu.VMEM((HALF_ROWS, cols), f32), pltpu.VMEM((HALF_ROWS, BLOCK), f32)],
    )


def grad_kernel(half, ids, e_in, w_in, mine, merged, grad, loss, work):
    def stat(k):
        return merged[:, half, k * BLOCK : (k + 1) * BLOCK]

    def own_stat(k):
        return mine[0, half : half + 1, k * BLOCK : (k + 1) * BLOCK]

    teacher_top = jnp.max(stat(0), axis=0, keepdims=True)
    teacher_scale = jnp.exp(stat(0) - teacher_top)
    teacher_total = jnp.sum(stat(1) * teacher_scale, axis=0, keepdims=True)
    gap = jnp.sum(stat(2) * teacher_scale, axis=0, keepdims=True)
    student_top = jnp.max(stat(3), axis=0, keepdims=True)
    student_total = jnp.sum(stat(4) * jnp.exp(stat(3) - student_top), axis=0, keepdims=True)
    loss_row = (gap / teacher_total - teacher_top - jnp.log(teacher_total)) + (
        student_top + jnp.log(student_total)
    )
    loss[...] = jnp.broadcast_to(loss_row, loss.shape)
    student_factor = loss_scale * jnp.exp(own_stat(3) - student_top) / student_total
    teacher_factor = loss_scale * jnp.exp(own_stat(0) - teacher_top) / teacher_total
    line = lax.broadcasted_iota(jnp.int32, (HALF_ROWS, BLOCK), 0)
    factors = jnp.where(line == 0, student_factor, jnp.where(line == 1, teacher_factor, 0.0)).T
    work[...] = e_in[...] * factors[:, 0:1]
    for r in range(ROW_BLOCKS):
        rows = slice(r * GROUP, (r + 1) * GROUP)
        factor = factors[rows, 1:2]
        for m in range(MOST):
            slot = r * MOST + m
            cols = pl.ds(pl.multiple_of(ids[slot] * BLOCK, BLOCK), BLOCK)
            work[rows, cols] = work[rows, cols] - factor * w_in[slot]
    grad[...] = work[...].astype(bf16)


def logit_grads(half, ids, e_in, w_in, mine, merged):
    return call(
        functools.partial(grad_kernel, half),
        [ids],
        [e_in, w_in, mine, merged],
        [(e_in.shape, bf16), ((8, BLOCK), f32)],
        [pltpu.VMEM(e_in.shape, f32)],
    )


def hidden_kernel(owners, targets, far, nxt, prv, own, turned_head, *refs):
    *outs, give, rows, work = refs
    for place, piece in enumerate((far, nxt, prv, own)):
        rows[place * HALF_ROWS : (place + 1) * HALF_ROWS, :] = piece[...]
    for part in (1, 0):
        work[...] = jnp.dot(rows[...], turned_head[part], preferred_element_type=f32)
        for place in range(4):
            zl = owners[place]
            for k in range(4):
                for zh in range(2):
                    low = place * HALF_ROWS + zh * GROUP
                    at = pl.ds(pl.multiple_of(low + targets[k] * 32, GROUP), GROUP)
                    if part:
                        give[k, zh * 4 + zl] = work[at, :]
                    else:
                        outs[k][zh * 4 + zl] = work[at, :]


def hidden_partial(owners, targets, pieces, turned_head):
    width = turned_head.shape[2]
    return call(
        hidden_kernel,
        [owners, targets],
        [*pieces, turned_head],
        [((8, GROUP, width), f32)] * 4 + [((4, 8, GROUP, width), f32)],
        [pltpu.VMEM((4 * HALF_ROWS, pieces[0].shape[1]), bf16), pltpu.VMEM((4 * HALF_ROWS, width), f32)],
    )


def head_kernel(turned_hidden, *refs):
    pieces = refs[:8]
    out, grads = refs[8:]
    for k in range(8):
        grads[k * HALF_ROWS : (k + 1) * HALF_ROWS, :] = pieces[k][...]
    step = 256
    for low in range(0, out.shape[1], step):
        cols = slice(low, low + step)
        out[:, cols] = jnp.dot(turned_hidden[...], grads[:, cols], preferred_element_type=f32).astype(bf16)


def head_total(turned_hidden, pieces):
    depth, tokens = turned_hidden.shape
    cols = pieces[0].shape[1]
    return call(
        head_kernel,
        [],
        [turned_hidden, *pieces],
        [((depth, cols), bf16)],
        [pltpu.VMEM((tokens, cols), bf16)],
    )[0]


def after(earlier, arrays):
    return lax.optimization_barrier((earlier, arrays))[1]


def shift(array, axis, step):
    size = lax.axis_size(axis)
    return lax.ppermute(array, axis, [(k, (k + step) % size) for k in range(size)])


def slots_of(kept, first, blocks):
    before = jnp.sum((kept < first).astype(jnp.int32), axis=1)
    place = jnp.arange(kept.shape[1], dtype=jnp.int32)
    wanted = before[:, None] + jnp.arange(MOST, dtype=jnp.int32)[None, :]
    chosen = (place[None, None, :] == wanted[:, :, None]) & (kept < first + blocks)[:, None, :]
    ids = jnp.sum(jnp.where(chosen, kept[:, None, :] - first, 0), axis=2)
    valid = jnp.any(chosen, axis=2)
    return ids.reshape(-1), valid.astype(jnp.int32).reshape(-1)


def body(teacher_hidden, teacher_head, student_hidden, student_head, kept):
    blocks = teacher_head.shape[1] // BLOCK
    x, c = lax.axis_index("x"), lax.axis_index("c")
    around = jnp.array([2, 1, 3, 0], jnp.int32)
    owners = ((x + around) % 4).astype(jnp.int32)
    targets = ((lax.axis_index("y") + around) % 4).astype(jnp.int32)
    core = jnp.stack([c, 1 - c]).astype(jnp.int32)
    ids, valid = slots_of(kept, lax.axis_index(VOCAB) * blocks, blocks)

    def to_both(to_next, to_prev):
        return shift(to_next, "x", 1), shift(to_prev, "x", -1)

    far_l, far_r = student_far(owners, student_hidden, student_head)
    nxt0, prv0, own0, nxt1, prv1, own1 = student_near(
        owners, *after(far_r, (student_hidden, student_head))
    )
    tfar_l, tfar_r, tnxt, tprv, town = teacher_partial(
        owners, ids, valid, *after(own1, (teacher_hidden, teacher_head))
    )
    far, tfar = to_both(far_l, far_r), to_both(tfar_l, tfar_r)
    merged0 = merge(functools.partial(student_merge_kernel, 0), *after(town, (nxt0, prv0)), *far)
    tmerged = merge(teacher_merge_kernel, *after(merged0[0], (tnxt, tprv)), *tfar)
    merged1 = merge(
        functools.partial(student_merge_kernel, 1), *after(tmerged[0], (nxt1, prv1)), *far
    )
    logits0 = (own0, *to_both(*merged0))
    teacher = (town, *to_both(*tmerged))
    logits1 = (own1, *to_both(*merged1))
    turned_hidden, turned_head = turned(owners, core, *after(merged1[0], (student_hidden, student_head)))

    def spread(grad):
        return shift(grad, "x", 2), shift(grad, "x", -1), shift(grad, "x", 1), grad

    def row_sums(pieces):
        *keep, give = hidden_partial(owners, targets, pieces, turned_head)
        got = shift(give, "c", 1)
        sums = [part + got[k] for k, part in enumerate(keep)]
        arrived = [shift(part, "y", step) for part, step in zip(sums, (2, 1, 3))]
        return give, sums[3], arrived

    devices = lax.axis_size(VOCAB)
    nothing = jnp.zeros((8, BLOCK), f32)
    e0, w0, first = local_stats(
        0, ids, valid, after(turned_head, logits0), teacher, nothing, (8, BLOCK)
    )
    e1, w1, mine = local_stats(1, ids, valid, logits1, teacher, first, (devices, 2, STATS * BLOCK))
    every = lax.all_to_all(mine, VOCAB, 0, 0, tiled=True)
    grad0, loss0 = logit_grads(0, ids, e0, w0, mine, every)
    grad1, loss1 = logit_grads(1, ids, e1, w1, mine, after(grad0, every))
    pieces0, pieces1 = after(grad1, spread(grad0)), spread(grad1)
    give0, own_rows0, arrived0 = row_sums(pieces0)
    pieces1 = after(give0, pieces1)
    give1, own_rows1, arrived1 = row_sums(pieces1)
    loss = jnp.concatenate([loss0, loss1], axis=1)
    losses = [loss] + [shift(loss, "x", step) for step in (1, 2, 3)]
    head_grad = head_total(turned_hidden, (*pieces0, *pieces1))
    (head_grad, losses), arrived1 = lax.optimization_barrier(((head_grad, losses), arrived1))
    both = [
        own + part[0] + part[1] + part[2]
        for own, part in ((own_rows0, arrived0), (own_rows1, arrived1))
    ]
    both = jnp.concatenate(both, axis=1)
    both = lax.all_to_all(both, "z", 0, 0, tiled=True)
    both = both.sum(axis=0).astype(bf16)
    sum0, sum1 = both[:GROUP], both[GROUP:]
    keep = jnp.where(c == 0, sum0, sum1)
    got = shift(jnp.where(c == 0, sum1, sum0), "c", 1)
    low, high = jnp.where(c == 0, keep, got), jnp.where(c == 0, got, keep)
    hidden_grad = jnp.concatenate([low, high[:, BLOCK:]], axis=1)

    row = jnp.stack([part[0] for part in losses]).reshape(4, 2, 4, 2, GROUP)
    row = lax.dynamic_index_in_dim(row, x, 2, keepdims=False)
    row = jnp.take(row, (x - jnp.arange(4)) % 4, axis=0)
    loss_rows = row.transpose(2, 0, 1, 3).reshape(-1)
    return loss_rows, hidden_grad, head_grad


def solution(mesh):
    split = Mesh(mesh.devices.reshape(4, 4, 8, 2), ("x", "y", "z", "c"))
    in_specs = (P(None, "x"), P("x", VOCAB), P(None, "x"), P("x", VOCAB), P())
    out_specs = (P("x"), P(VOCAB, "x"), P("x", VOCAB))
    return jax.shard_map(body, mesh=split, in_specs=in_specs, out_specs=out_specs, check_vma=False)
```

```python
import functools

import jax
import jax.numpy as jnp
from jax import lax
from jax.experimental import pallas as pl
from jax.experimental.pallas import tpu as pltpu
from jax.sharding import Mesh
from jax.sharding import PartitionSpec as P

VOCAB = ("y", "z", "c")
BLOCK = 128
MOST = 4
GROUP = 16
ROW_BLOCKS = 8
SLOTS = ROW_BLOCKS * MOST
STATS = 5
HALF_ROWS = ROW_BLOCKS * GROUP

masked_value = -1e30
loss_scale = 2048.0
f32 = jnp.float32
bf16 = jnp.bfloat16
MIB = 1024 * 1024


def whole(shape):
    return pl.BlockSpec(shape, lambda i: (0,) * len(shape))


def call(kernel, scalars, arrays, outs, scratch=(), limit=30):
    return pl.pallas_call(
        kernel,
        grid=(1,),
        in_specs=[pl.BlockSpec(memory_space=pltpu.SMEM)] * len(scalars)
        + [whole(array.shape) for array in arrays],
        out_specs=[whole(shape) for shape, _ in outs],
        out_shape=[jax.ShapeDtypeStruct(shape, dtype) for shape, dtype in outs],
        scratch_shapes=list(scratch),
        compiler_params=pltpu.CompilerParams(vmem_limit_bytes=limit * MIB),
    )(*scalars, *arrays)


def group_rows(row_block, owner, half):
    return pl.ds(pl.multiple_of(row_block * BLOCK + owner * 32 + half * GROUP, GROUP), GROUP)


def teacher_slots(owners, ids, valid, hidden, head, lhs, store):
    def row_block(r, carry):
        for place in range(4):
            rows = pl.ds(pl.multiple_of(r * BLOCK + owners[place] * 32, 32), 32)
            lhs[place * 32 : (place + 1) * 32, :] = hidden[rows, :]
        rows = pl.ds(pl.multiple_of(r * GROUP, GROUP), GROUP)
        for m in range(MOST):
            slot = r * MOST + m

            @pl.when(valid[slot] > 0)
            def _():
                cols = pl.ds(pl.multiple_of(ids[slot] * BLOCK, BLOCK), BLOCK)
                part = jnp.dot(lhs[...], head[:, cols], preferred_element_type=f32)
                for place in range(4):
                    store(rows, m, place, part[place * 32 : (place + 1) * 32])

        return carry

    lax.fori_loop(0, ROW_BLOCKS, row_block, 0)


def gather_rows(owners, hidden, lhs, places=range(4)):
    low = 0
    for half in range(2):
        for place in places:
            for r in range(ROW_BLOCKS):
                lhs[low : low + GROUP, :] = hidden[group_rows(r, owners[place], half), :]
                low += GROUP


def student_far_kernel(owners, hidden, head, far_l, far_r, lhs):
    gather_rows(owners, hidden, lhs, (0,))
    width = far_l.shape[2]
    for side, far in enumerate((far_l, far_r)):
        cols = slice(side * width, (side + 1) * width)
        part = jnp.dot(lhs[...], head[:, cols], preferred_element_type=f32)
        far[0] = part[:HALF_ROWS]
        far[1] = part[HALF_ROWS:]


def student_far(owners, hidden, head):
    tokens, depth = hidden.shape
    return call(
        student_far_kernel,
        [owners],
        [hidden, head],
        [((2, HALF_ROWS, head.shape[1] // 2), f32)] * 2,
        [pltpu.VMEM((tokens // 4, depth), bf16)],
    )


def student_near_kernel(owners, hidden, head, nxt0, prv0, own0, nxt1, prv1, own1, lhs):
    gather_rows(owners, hidden, lhs, (1, 2, 3))
    width = head.shape[1] // 2
    for half, wide in enumerate(((nxt0, prv0, own0), (nxt1, prv1, own1))):
        rows = slice(half * 3 * HALF_ROWS, (half + 1) * 3 * HALF_ROWS)
        for side in range(2):
            cols = slice(side * width, (side + 1) * width)
            part = jnp.dot(lhs[rows], head[:, cols], preferred_element_type=f32)
            for place, ref in enumerate(wide):
                ref[:, cols] = part[place * HALF_ROWS : (place + 1) * HALF_ROWS]


def student_near(owners, hidden, head):
    tokens, depth = hidden.shape
    return call(
        student_near_kernel,
        [owners],
        [hidden, head],
        [((HALF_ROWS, head.shape[1]), f32)] * 6,
        [pltpu.VMEM((tokens // 4 * 3, depth), bf16)],
    )


def teacher_kernel(owners, ids, valid, hidden, head, far_l, far_r, nxt, prv, own, lhs):
    wide = (nxt, prv, own)
    for ref in (far_l, far_r, *wide):
        ref[...] = jnp.zeros(ref.shape, f32)

    def store(rows, m, place, part):
        for half in range(2):
            value = part[half * GROUP : (half + 1) * GROUP]
            if place == 0:
                low = (m % 2) * BLOCK
                (far_l, far_r)[m // 2][half, rows, low : low + BLOCK] = value
            else:
                wide[place - 1][half, rows, m * BLOCK : (m + 1) * BLOCK] = value

    teacher_slots(owners, ids, valid, hidden, head, lhs, store)


def teacher_partial(owners, ids, valid, hidden, head):
    return call(
        teacher_kernel,
        [owners, ids, valid],
        [hidden, head],
        [((2, HALF_ROWS, 2 * BLOCK), f32)] * 2 + [((2, HALF_ROWS, MOST * BLOCK), f32)] * 3,
        [pltpu.VMEM((BLOCK, head.shape[0]), bf16)],
    )


def student_merge_kernel(half, nxt, prv, from_prev, from_next, to_next, to_prev):
    cut = from_prev.shape[2]
    to_next[:, :cut] = nxt[:, :cut] + from_prev[half]
    to_next[:, cut:] = nxt[:, cut:]
    to_prev[:, :cut] = prv[:, :cut]
    to_prev[:, cut:] = prv[:, cut:] + from_next[half]


def teacher_merge_kernel(nxt, prv, from_prev, from_next, to_next, to_prev):
    cut = from_prev.shape[2]
    to_next[:, :, :cut] = nxt[:, :, :cut] + from_prev[...]
    to_next[:, :, cut:] = nxt[:, :, cut:]
    to_prev[:, :, :cut] = prv[:, :, :cut]
    to_prev[:, :, cut:] = prv[:, :, cut:] + from_next[...]


def merge(kernel, *parts):
    return call(kernel, [], parts, [(parts[0].shape, f32)] * 2)


def turn_kernel(owners, core, hidden, head, turned_hidden, turned_head, lhs):
    gather_rows(owners, hidden, lhs)
    turned_hidden[...] = lhs[...].T
    for part in range(2):
        rows = pl.ds(pl.multiple_of(core[part] * 384, 128), 512)
        turned_head[part] = head[rows, :].T


def turned(owners, core, hidden, head):
    return call(
        turn_kernel,
        [owners, core],
        [hidden, head],
        [((hidden.shape[1], hidden.shape[0]), bf16), ((2, head.shape[1], 512), bf16)],
        [pltpu.VMEM(hidden.shape, bf16)],
    )


def stats_kernel(half, ids, valid, own, from_prev, from_next, town, tprev, tnext, first, e_out, w_out, stats, logits, tile):
    lane = lax.broadcasted_iota(jnp.int32, (GROUP, BLOCK), 1)
    for r in range(ROW_BLOCKS):
        rows = slice(r * GROUP, (r + 1) * GROUP)
        student = own[rows] + from_prev[rows] + from_next[rows]
        logits[rows] = student
        student_top = jnp.max(student, axis=1, keepdims=True)
        student_exp = jnp.exp(student - student_top)
        e_out[rows] = student_exp
        student_total = jnp.sum(student_exp, axis=1, keepdims=True)
        teacher = []
        for m in range(MOST):
            cols = slice(m * BLOCK, (m + 1) * BLOCK)
            value = town[half, rows, cols] + tprev[half, rows, cols] + tnext[half, rows, cols]
            teacher.append(jnp.where(valid[r * MOST + m] > 0, value, masked_value))
        highest = functools.reduce(jnp.maximum, teacher)
        teacher_top = jnp.max(highest, axis=1, keepdims=True)
        total = gap = jnp.zeros((GROUP, BLOCK), f32)
        for m in range(MOST):
            slot = r * MOST + m
            weight = jnp.where(valid[slot] > 0, jnp.exp(teacher[m] - teacher_top), 0.0)
            w_out[slot] = weight
            cols = pl.ds(pl.multiple_of(ids[slot] * BLOCK, BLOCK), BLOCK)
            total += weight
            gap += weight * (teacher[m] - logits[rows, cols])
        columns = (
            teacher_top,
            jnp.sum(total, axis=1, keepdims=True),
            jnp.sum(gap, axis=1, keepdims=True),
            student_top,
            student_total,
        )
        line = jnp.zeros((GROUP, BLOCK), f32)
        for k, column in enumerate(columns):
            line = jnp.where(lane == k, column, line)
        tile[rows] = line
    if half == 0:
        stats[...] = tile[...].T[:8]
    else:
        both = (first[...], tile[...].T[:8])
        lines = [jnp.concatenate([part[k : k + 1] for k in range(STATS)], axis=1) for part in both]
        stats[...] = jnp.broadcast_to(jnp.concatenate(lines, axis=0)[None], stats.shape)


def local_stats(half, ids, valid, student, teacher, first, sent):
    cols = student[0].shape[1]
    return call(
        functools.partial(stats_kernel, half),
        [ids, valid],
        [*student, *teacher, first],
        [((HALF_ROWS, cols), f32), ((SLOTS, GROUP, BLOCK), f32), (sent, f32)],
        [pltpu.VMEM((HALF_ROWS, cols), f32), pltpu.VMEM((HALF_ROWS, BLOCK), f32)],
    )


def grad_kernel(half, ids, e_in, w_in, mine, merged, grad, loss, work):
    def stat(k):
        return merged[:, half, k * BLOCK : (k + 1) * BLOCK]

    def own_stat(k):
        return mine[0, half : half + 1, k * BLOCK : (k + 1) * BLOCK]

    teacher_top = jnp.max(stat(0), axis=0, keepdims=True)
    teacher_scale = jnp.exp(stat(0) - teacher_top)
    teacher_total = jnp.sum(stat(1) * teacher_scale, axis=0, keepdims=True)
    gap = jnp.sum(stat(2) * teacher_scale, axis=0, keepdims=True)
    student_top = jnp.max(stat(3), axis=0, keepdims=True)
    student_total = jnp.sum(stat(4) * jnp.exp(stat(3) - student_top), axis=0, keepdims=True)
    loss_row = (gap / teacher_total - teacher_top - jnp.log(teacher_total)) + (
        student_top + jnp.log(student_total)
    )
    loss[...] = jnp.broadcast_to(loss_row, loss.shape)
    student_factor = loss_scale * jnp.exp(own_stat(3) - student_top) / student_total
    teacher_factor = loss_scale * jnp.exp(own_stat(0) - teacher_top) / teacher_total
    line = lax.broadcasted_iota(jnp.int32, (HALF_ROWS, BLOCK), 0)
    factors = jnp.where(line == 0, student_factor, jnp.where(line == 1, teacher_factor, 0.0)).T
    work[...] = e_in[...] * factors[:, 0:1]
    for r in range(ROW_BLOCKS):
        rows = slice(r * GROUP, (r + 1) * GROUP)
        factor = factors[rows, 1:2]
        for m in range(MOST):
            slot = r * MOST + m
            cols = pl.ds(pl.multiple_of(ids[slot] * BLOCK, BLOCK), BLOCK)
            work[rows, cols] = work[rows, cols] - factor * w_in[slot]
    grad[...] = work[...].astype(bf16)


def logit_grads(half, ids, e_in, w_in, mine, merged):
    return call(
        functools.partial(grad_kernel, half),
        [ids],
        [e_in, w_in, mine, merged],
        [(e_in.shape, bf16), ((8, BLOCK), f32)],
        [pltpu.VMEM(e_in.shape, f32)],
    )


def hidden_kernel(owners, targets, far, nxt, prv, own, turned_head, *refs):
    outs, gives, (rows, work) = refs[:4], refs[4:8], refs[8:]
    for place, piece in enumerate((far, nxt, prv, own)):
        rows[place * HALF_ROWS : (place + 1) * HALF_ROWS, :] = piece[...]
    for part in (1, 0):
        work[...] = jnp.dot(rows[...], turned_head[part], preferred_element_type=f32)
        for place in range(4):
            zl = owners[place]
            for k in range(4):
                for zh in range(2):
                    low = place * HALF_ROWS + zh * GROUP
                    at = pl.ds(pl.multiple_of(low + targets[k] * 32, GROUP), GROUP)
                    if part:
                        gives[k][zh * 4 + zl] = work[at, :]
                    else:
                        outs[k][zh * 4 + zl] = work[at, :]


def hidden_partial(owners, targets, pieces, turned_head):
    width = turned_head.shape[2]
    return call(
        hidden_kernel,
        [owners, targets],
        [*pieces, turned_head],
        [((8, GROUP, width), f32)] * 8,
        [pltpu.VMEM((4 * HALF_ROWS, pieces[0].shape[1]), bf16), pltpu.VMEM((4 * HALF_ROWS, width), f32)],
    )


def head_kernel(turned_hidden, *refs):
    pieces = refs[:8]
    out, grads = refs[8:]
    for k in range(8):
        grads[k * HALF_ROWS : (k + 1) * HALF_ROWS, :] = pieces[k][...]
    step = 256
    for low in range(0, out.shape[1], step):
        cols = slice(low, low + step)
        out[:, cols] = jnp.dot(turned_hidden[...], grads[:, cols], preferred_element_type=f32).astype(bf16)


def head_total(turned_hidden, pieces):
    depth, tokens = turned_hidden.shape
    cols = pieces[0].shape[1]
    return call(
        head_kernel,
        [],
        [turned_hidden, *pieces],
        [((depth, cols), bf16)],
        [pltpu.VMEM((tokens, cols), bf16)],
    )[0]


def after(earlier, arrays):
    return lax.optimization_barrier((earlier, arrays))[1]


def shift(array, axis, step):
    size = lax.axis_size(axis)
    return lax.ppermute(array, axis, [(k, (k + step) % size) for k in range(size)])


def slots_of(kept, first, blocks):
    before = jnp.sum((kept < first).astype(jnp.int32), axis=1)
    place = jnp.arange(kept.shape[1], dtype=jnp.int32)
    wanted = before[:, None] + jnp.arange(MOST, dtype=jnp.int32)[None, :]
    chosen = (place[None, None, :] == wanted[:, :, None]) & (kept < first + blocks)[:, None, :]
    ids = jnp.sum(jnp.where(chosen, kept[:, None, :] - first, 0), axis=2)
    valid = jnp.any(chosen, axis=2)
    return ids.reshape(-1), valid.astype(jnp.int32).reshape(-1)


def body(teacher_hidden, teacher_head, student_hidden, student_head, kept):
    blocks = teacher_head.shape[1] // BLOCK
    x, c = lax.axis_index("x"), lax.axis_index("c")
    around = jnp.array([2, 1, 3, 0], jnp.int32)
    owners = ((x + around) % 4).astype(jnp.int32)
    targets = ((lax.axis_index("y") + around) % 4).astype(jnp.int32)
    core = jnp.stack([c, 1 - c]).astype(jnp.int32)
    ids, valid = slots_of(kept, lax.axis_index(VOCAB) * blocks, blocks)

    def to_both(to_next, to_prev):
        return shift(to_next, "x", 1), shift(to_prev, "x", -1)

    far_l, far_r = student_far(owners, student_hidden, student_head)
    nxt0, prv0, own0, nxt1, prv1, own1 = student_near(
        owners, *after(far_r, (student_hidden, student_head))
    )
    tfar_l, tfar_r, tnxt, tprv, town = teacher_partial(
        owners, ids, valid, *after(own1, (teacher_hidden, teacher_head))
    )
    far, tfar = to_both(far_l, far_r), to_both(tfar_l, tfar_r)
    merged0 = merge(functools.partial(student_merge_kernel, 0), *after(town, (nxt0, prv0)), *far)
    tmerged = merge(teacher_merge_kernel, *after(merged0[0], (tnxt, tprv)), *tfar)
    merged1 = merge(
        functools.partial(student_merge_kernel, 1), *after(tmerged[0], (nxt1, prv1)), *far
    )
    logits0 = (own0, *to_both(*merged0))
    teacher = (town, *to_both(*tmerged))
    logits1 = (own1, *to_both(*merged1))
    turned_hidden, turned_head = turned(owners, core, *after(merged1[0], (student_hidden, student_head)))

    def spread(grad):
        return shift(grad, "x", 2), shift(grad, "x", -1), shift(grad, "x", 1), grad

    def row_sums(pieces):
        parts = hidden_partial(owners, targets, pieces, turned_head)
        sums = [part + shift(give, "c", 1) for part, give in zip(parts[:4], parts[4:])]
        arrived = [shift(part, "y", step) for part, step in zip(sums, (2, 1, 3))]
        return sums, sums[3], arrived

    devices = lax.axis_size(VOCAB)
    nothing = jnp.zeros((8, BLOCK), f32)
    e0, w0, first = local_stats(
        0, ids, valid, after(turned_head, logits0), teacher, nothing, (8, BLOCK)
    )
    e1, w1, mine = local_stats(1, ids, valid, logits1, teacher, first, (devices, 2, STATS * BLOCK))
    every = lax.all_to_all(mine, VOCAB, 0, 0, tiled=True)
    grad0, loss0 = logit_grads(0, ids, e0, w0, mine, every)
    grad1, loss1 = logit_grads(1, ids, e1, w1, mine, after(grad0, every))
    pieces0, pieces1 = after(grad1, spread(grad0)), spread(grad1)
    give0, own_rows0, arrived0 = row_sums(pieces0)
    pieces1 = after(give0, pieces1)
    give1, own_rows1, arrived1 = row_sums(pieces1)
    loss = jnp.concatenate([loss0, loss1], axis=1)
    losses = [loss] + [shift(loss, "x", step) for step in (1, 2, 3)]
    head_grad = head_total(turned_hidden, (*pieces0, *pieces1))
    (head_grad, losses), arrived1 = lax.optimization_barrier(((head_grad, losses), arrived1))
    both = [
        own + part[0] + part[1] + part[2]
        for own, part in ((own_rows0, arrived0), (own_rows1, arrived1))
    ]
    both = jnp.concatenate(both, axis=1)
    both = lax.all_to_all(both, "z", 0, 0, tiled=True)
    both = both.sum(axis=0).astype(bf16)
    sum0, sum1 = both[:GROUP], both[GROUP:]
    keep = jnp.where(c == 0, sum0, sum1)
    got = shift(jnp.where(c == 0, sum1, sum0), "c", 1)
    low, high = jnp.where(c == 0, keep, got), jnp.where(c == 0, got, keep)
    hidden_grad = jnp.concatenate([low, high[:, BLOCK:]], axis=1)

    row = jnp.stack([part[0] for part in losses]).reshape(4, 2, 4, 2, GROUP)
    row = lax.dynamic_index_in_dim(row, x, 2, keepdims=False)
    row = jnp.take(row, (x - jnp.arange(4)) % 4, axis=0)
    loss_rows = row.transpose(2, 0, 1, 3).reshape(-1)
    return loss_rows, hidden_grad, head_grad


def solution(mesh):
    split = Mesh(mesh.devices.reshape(4, 4, 8, 2), ("x", "y", "z", "c"))
    in_specs = (P(None, "x"), P("x", VOCAB), P(None, "x"), P("x", VOCAB), P())
    out_specs = (P("x"), P(VOCAB, "x"), P("x", VOCAB))
    return jax.shard_map(body, mesh=split, in_specs=in_specs, out_specs=out_specs, check_vma=False)
```

```python
import functools

import jax
import jax.numpy as jnp
from jax import lax
from jax.experimental import pallas as pl
from jax.experimental.pallas import tpu as pltpu
from jax.sharding import Mesh
from jax.sharding import PartitionSpec as P

VOCAB = ("y", "z", "c")
BLOCK = 128
MOST = 4
GROUP = 16
ROW_BLOCKS = 8
SLOTS = ROW_BLOCKS * MOST
STATS = 5
HALF_ROWS = ROW_BLOCKS * GROUP

masked_value = -1e30
loss_scale = 2048.0
f32 = jnp.float32
bf16 = jnp.bfloat16
MIB = 1024 * 1024


def whole(shape):
    return pl.BlockSpec(shape, lambda i: (0,) * len(shape))


def call(kernel, scalars, arrays, outs, scratch=(), limit=30):
    return pl.pallas_call(
        kernel,
        grid=(1,),
        in_specs=[pl.BlockSpec(memory_space=pltpu.SMEM)] * len(scalars)
        + [whole(array.shape) for array in arrays],
        out_specs=[whole(shape) for shape, _ in outs],
        out_shape=[jax.ShapeDtypeStruct(shape, dtype) for shape, dtype in outs],
        scratch_shapes=list(scratch),
        compiler_params=pltpu.CompilerParams(vmem_limit_bytes=limit * MIB),
    )(*scalars, *arrays)


def group_rows(row_block, owner, half):
    return pl.ds(pl.multiple_of(row_block * BLOCK + owner * 32 + half * GROUP, GROUP), GROUP)


def teacher_slots(owners, ids, valid, hidden, head, lhs, store):
    def row_block(r, carry):
        for place in range(4):
            rows = pl.ds(pl.multiple_of(r * BLOCK + owners[place] * 32, 32), 32)
            lhs[place * 32 : (place + 1) * 32, :] = hidden[rows, :]
        rows = pl.ds(pl.multiple_of(r * GROUP, GROUP), GROUP)
        for m in range(MOST):
            slot = r * MOST + m

            @pl.when(valid[slot] > 0)
            def _():
                cols = pl.ds(pl.multiple_of(ids[slot] * BLOCK, BLOCK), BLOCK)
                part = jnp.dot(lhs[...], head[:, cols], preferred_element_type=f32)
                for place in range(4):
                    store(rows, m, place, part[place * 32 : (place + 1) * 32])

        return carry

    lax.fori_loop(0, ROW_BLOCKS, row_block, 0)


def gather_rows(owners, hidden, lhs, places=range(4)):
    low = 0
    for half in range(2):
        for place in places:
            for r in range(ROW_BLOCKS):
                lhs[low : low + GROUP, :] = hidden[group_rows(r, owners[place], half), :]
                low += GROUP


def student_far_kernel(owners, hidden, head, far_l, far_r, lhs):
    gather_rows(owners, hidden, lhs, (0,))
    width = far_l.shape[2]
    for side, far in enumerate((far_l, far_r)):
        cols = slice(side * width, (side + 1) * width)
        part = jnp.dot(lhs[...], head[:, cols], preferred_element_type=f32)
        far[0] = part[:HALF_ROWS]
        far[1] = part[HALF_ROWS:]


def student_far(owners, hidden, head):
    tokens, depth = hidden.shape
    return call(
        student_far_kernel,
        [owners],
        [hidden, head],
        [((2, HALF_ROWS, head.shape[1] // 2), f32)] * 2,
        [pltpu.VMEM((tokens // 4, depth), bf16)],
    )


def student_near_kernel(owners, hidden, head, nxt0, prv0, own0, nxt1, prv1, own1, lhs):
    gather_rows(owners, hidden, lhs, (1, 2, 3))
    width = head.shape[1] // 2
    for half, wide in enumerate(((nxt0, prv0, own0), (nxt1, prv1, own1))):
        rows = slice(half * 3 * HALF_ROWS, (half + 1) * 3 * HALF_ROWS)
        for side in range(2):
            cols = slice(side * width, (side + 1) * width)
            part = jnp.dot(lhs[rows], head[:, cols], preferred_element_type=f32)
            for place, ref in enumerate(wide):
                ref[:, cols] = part[place * HALF_ROWS : (place + 1) * HALF_ROWS]


def student_near(owners, hidden, head):
    tokens, depth = hidden.shape
    return call(
        student_near_kernel,
        [owners],
        [hidden, head],
        [((HALF_ROWS, head.shape[1]), f32)] * 6,
        [pltpu.VMEM((tokens // 4 * 3, depth), bf16)],
    )


def teacher_kernel(owners, ids, valid, hidden, head, far_l, far_r, nxt, prv, own, lhs):
    wide = (nxt, prv, own)
    for ref in (far_l, far_r, *wide):
        ref[...] = jnp.zeros(ref.shape, f32)

    def store(rows, m, place, part):
        for half in range(2):
            value = part[half * GROUP : (half + 1) * GROUP]
            if place == 0:
                low = (m % 2) * BLOCK
                (far_l, far_r)[m // 2][half, rows, low : low + BLOCK] = value
            else:
                wide[place - 1][half, rows, m * BLOCK : (m + 1) * BLOCK] = value

    teacher_slots(owners, ids, valid, hidden, head, lhs, store)


def teacher_partial(owners, ids, valid, hidden, head):
    return call(
        teacher_kernel,
        [owners, ids, valid],
        [hidden, head],
        [((2, HALF_ROWS, 2 * BLOCK), f32)] * 2 + [((2, HALF_ROWS, MOST * BLOCK), f32)] * 3,
        [pltpu.VMEM((BLOCK, head.shape[0]), bf16)],
    )


def student_merge_kernel(half, nxt, prv, from_prev, from_next, to_next, to_prev):
    cut = from_prev.shape[2]
    to_next[:, :cut] = nxt[:, :cut] + from_prev[half]
    to_next[:, cut:] = nxt[:, cut:]
    to_prev[:, :cut] = prv[:, :cut]
    to_prev[:, cut:] = prv[:, cut:] + from_next[half]


def teacher_merge_kernel(nxt, prv, from_prev, from_next, to_next, to_prev):
    cut = from_prev.shape[2]
    to_next[:, :, :cut] = nxt[:, :, :cut] + from_prev[...]
    to_next[:, :, cut:] = nxt[:, :, cut:]
    to_prev[:, :, :cut] = prv[:, :, :cut]
    to_prev[:, :, cut:] = prv[:, :, cut:] + from_next[...]


def merge(kernel, *parts):
    return call(kernel, [], parts, [(parts[0].shape, f32)] * 2)


def turn_kernel(owners, core, hidden, head, turned_hidden, turned_head, lhs):
    gather_rows(owners, hidden, lhs)
    turned_hidden[...] = lhs[...].T
    for part in range(2):
        rows = pl.ds(pl.multiple_of(core[part] * 384, 128), 512)
        turned_head[part] = head[rows, :].T


def turned(owners, core, hidden, head):
    return call(
        turn_kernel,
        [owners, core],
        [hidden, head],
        [((hidden.shape[1], hidden.shape[0]), bf16), ((2, head.shape[1], 512), bf16)],
        [pltpu.VMEM(hidden.shape, bf16)],
    )


def stats_kernel(half, ids, valid, own, from_prev, from_next, town, tprev, tnext, first, e_out, w_out, stats, logits, tile):
    lane = lax.broadcasted_iota(jnp.int32, (GROUP, BLOCK), 1)
    for r in range(ROW_BLOCKS):
        rows = slice(r * GROUP, (r + 1) * GROUP)
        student = own[rows] + from_prev[rows] + from_next[rows]
        logits[rows] = student
        student_top = jnp.max(student, axis=1, keepdims=True)
        student_exp = jnp.exp(student - student_top)
        e_out[rows] = student_exp
        student_total = jnp.sum(student_exp, axis=1, keepdims=True)
        teacher = []
        for m in range(MOST):
            cols = slice(m * BLOCK, (m + 1) * BLOCK)
            value = town[half, rows, cols] + tprev[half, rows, cols] + tnext[half, rows, cols]
            teacher.append(jnp.where(valid[r * MOST + m] > 0, value, masked_value))
        highest = functools.reduce(jnp.maximum, teacher)
        teacher_top = jnp.max(highest, axis=1, keepdims=True)
        total = gap = jnp.zeros((GROUP, BLOCK), f32)
        for m in range(MOST):
            slot = r * MOST + m
            weight = jnp.where(valid[slot] > 0, jnp.exp(teacher[m] - teacher_top), 0.0)
            w_out[slot] = weight
            cols = pl.ds(pl.multiple_of(ids[slot] * BLOCK, BLOCK), BLOCK)
            total += weight
            gap += weight * (teacher[m] - logits[rows, cols])
        columns = (
            teacher_top,
            jnp.sum(total, axis=1, keepdims=True),
            jnp.sum(gap, axis=1, keepdims=True),
            student_top,
            student_total,
        )
        line = jnp.zeros((GROUP, BLOCK), f32)
        for k, column in enumerate(columns):
            line = jnp.where(lane == k, column, line)
        tile[rows] = line
    if half == 0:
        stats[...] = tile[...].T[:8]
    else:
        both = (first[...], tile[...].T[:8])
        lines = [jnp.concatenate([part[k : k + 1] for k in range(STATS)], axis=1) for part in both]
        stats[...] = jnp.broadcast_to(jnp.concatenate(lines, axis=0)[None], stats.shape)


def local_stats(half, ids, valid, student, teacher, first, sent):
    cols = student[0].shape[1]
    return call(
        functools.partial(stats_kernel, half),
        [ids, valid],
        [*student, *teacher, first],
        [((HALF_ROWS, cols), f32), ((SLOTS, GROUP, BLOCK), f32), (sent, f32)],
        [pltpu.VMEM((HALF_ROWS, cols), f32), pltpu.VMEM((HALF_ROWS, BLOCK), f32)],
    )


def grad_kernel(half, ids, e_in, w_in, mine, merged, grad, loss, work):
    def stat(k):
        return merged[:, half, k * BLOCK : (k + 1) * BLOCK]

    def own_stat(k):
        return mine[0, half : half + 1, k * BLOCK : (k + 1) * BLOCK]

    teacher_top = jnp.max(stat(0), axis=0, keepdims=True)
    teacher_scale = jnp.exp(stat(0) - teacher_top)
    teacher_total = jnp.sum(stat(1) * teacher_scale, axis=0, keepdims=True)
    gap = jnp.sum(stat(2) * teacher_scale, axis=0, keepdims=True)
    student_top = jnp.max(stat(3), axis=0, keepdims=True)
    student_total = jnp.sum(stat(4) * jnp.exp(stat(3) - student_top), axis=0, keepdims=True)
    loss_row = (gap / teacher_total - teacher_top - jnp.log(teacher_total)) + (
        student_top + jnp.log(student_total)
    )
    loss[...] = jnp.broadcast_to(loss_row, loss.shape)
    student_factor = loss_scale * jnp.exp(own_stat(3) - student_top) / student_total
    teacher_factor = loss_scale * jnp.exp(own_stat(0) - teacher_top) / teacher_total
    line = lax.broadcasted_iota(jnp.int32, (HALF_ROWS, BLOCK), 0)
    factors = jnp.where(line == 0, student_factor, jnp.where(line == 1, teacher_factor, 0.0)).T
    work[...] = e_in[...] * factors[:, 0:1]
    for r in range(ROW_BLOCKS):
        rows = slice(r * GROUP, (r + 1) * GROUP)
        factor = factors[rows, 1:2]
        for m in range(MOST):
            slot = r * MOST + m
            cols = pl.ds(pl.multiple_of(ids[slot] * BLOCK, BLOCK), BLOCK)
            work[rows, cols] = work[rows, cols] - factor * w_in[slot]
    grad[...] = work[...].astype(bf16)


def logit_grads(half, ids, e_in, w_in, mine, merged):
    return call(
        functools.partial(grad_kernel, half),
        [ids],
        [e_in, w_in, mine, merged],
        [(e_in.shape, bf16), ((8, BLOCK), f32)],
        [pltpu.VMEM(e_in.shape, f32)],
    )


def hidden_kernel(owners, targets, far, nxt, prv, own, turned_head, *refs):
    outs, gives, (rows, work) = refs[:4], refs[4:8], refs[8:]
    for place, piece in enumerate((far, nxt, prv, own)):
        rows[place * HALF_ROWS : (place + 1) * HALF_ROWS, :] = piece[...]
    for part in (1, 0):
        work[...] = jnp.dot(rows[...], turned_head[part], preferred_element_type=f32)
        for place in range(4):
            zl = owners[place]
            for k in range(4):
                for zh in range(2):
                    low = place * HALF_ROWS + zh * GROUP
                    at = pl.ds(pl.multiple_of(low + targets[k] * 32, GROUP), GROUP)
                    if part:
                        gives[k][zh * 4 + zl] = work[at, :]
                    else:
                        outs[k][zh * 4 + zl] = work[at, :]


def hidden_partial(owners, targets, pieces, turned_head):
    width = turned_head.shape[2]
    return call(
        hidden_kernel,
        [owners, targets],
        [*pieces, turned_head],
        [((8, GROUP, width), f32)] * 8,
        [pltpu.VMEM((4 * HALF_ROWS, pieces[0].shape[1]), bf16), pltpu.VMEM((4 * HALF_ROWS, width), f32)],
    )


def head_kernel(turned_hidden, *refs):
    pieces = refs[:8]
    out, grads = refs[8:]
    for k in range(8):
        grads[k * HALF_ROWS : (k + 1) * HALF_ROWS, :] = pieces[k][...]
    step = 256
    for low in range(0, out.shape[1], step):
        cols = slice(low, low + step)
        out[:, cols] = jnp.dot(turned_hidden[...], grads[:, cols], preferred_element_type=f32).astype(bf16)


def head_total(turned_hidden, pieces):
    depth, tokens = turned_hidden.shape
    cols = pieces[0].shape[1]
    return call(
        head_kernel,
        [],
        [turned_hidden, *pieces],
        [((depth, cols), bf16)],
        [pltpu.VMEM((tokens, cols), bf16)],
    )[0]


def after(earlier, arrays):
    return lax.optimization_barrier((earlier, arrays))[1]


def shift(array, axis, step):
    size = lax.axis_size(axis)
    return lax.ppermute(array, axis, [(k, (k + step) % size) for k in range(size)])


def slots_of(kept, first, blocks):
    before = jnp.sum((kept < first).astype(jnp.int32), axis=1)
    place = jnp.arange(kept.shape[1], dtype=jnp.int32)
    wanted = before[:, None] + jnp.arange(MOST, dtype=jnp.int32)[None, :]
    chosen = (place[None, None, :] == wanted[:, :, None]) & (kept < first + blocks)[:, None, :]
    ids = jnp.sum(jnp.where(chosen, kept[:, None, :] - first, 0), axis=2)
    valid = jnp.any(chosen, axis=2)
    return ids.reshape(-1), valid.astype(jnp.int32).reshape(-1)


def body(teacher_hidden, teacher_head, student_hidden, student_head, kept):
    blocks = teacher_head.shape[1] // BLOCK
    x, c = lax.axis_index("x"), lax.axis_index("c")
    around = jnp.array([2, 1, 3, 0], jnp.int32)
    owners = ((x + around) % 4).astype(jnp.int32)
    targets = ((lax.axis_index("y") + around) % 4).astype(jnp.int32)
    core = jnp.stack([c, 1 - c]).astype(jnp.int32)
    ids, valid = slots_of(kept, lax.axis_index(VOCAB) * blocks, blocks)

    def to_both(to_next, to_prev):
        return shift(to_next, "x", 1), shift(to_prev, "x", -1)

    far_l, far_r = student_far(owners, student_hidden, student_head)
    nxt0, prv0, own0, nxt1, prv1, own1 = student_near(
        after(far_r, owners), student_hidden, student_head
    )
    tfar_l, tfar_r, tnxt, tprv, town = teacher_partial(
        after(own1, owners), ids, valid, teacher_hidden, teacher_head
    )
    far, tfar = to_both(far_l, far_r), to_both(tfar_l, tfar_r)
    merged0 = merge(functools.partial(student_merge_kernel, 0), *after(town, (nxt0, prv0)), *far)
    tmerged = merge(teacher_merge_kernel, *after(merged0[0], (tnxt, tprv)), *tfar)
    merged1 = merge(
        functools.partial(student_merge_kernel, 1), *after(tmerged[0], (nxt1, prv1)), *far
    )
    logits0 = (own0, *to_both(*merged0))
    teacher = (town, *to_both(*tmerged))
    logits1 = (own1, *to_both(*merged1))
    turned_hidden, turned_head = turned(after(merged1[0], owners), core, student_hidden, student_head)

    def spread(grad):
        return shift(grad, "x", 2), shift(grad, "x", -1), shift(grad, "x", 1), grad

    def row_sums(pieces):
        parts = hidden_partial(owners, targets, pieces, turned_head)
        sums = [part + shift(give, "c", 1) for part, give in zip(parts[:4], parts[4:])]
        arrived = [shift(part, "y", step) for part, step in zip(sums, (2, 1, 3))]
        return sums, sums[3], arrived

    devices = lax.axis_size(VOCAB)
    nothing = jnp.zeros((8, BLOCK), f32)
    e0, w0, first = local_stats(
        0, ids, valid, after(turned_head, logits0), teacher, nothing, (8, BLOCK)
    )
    e1, w1, mine = local_stats(1, ids, valid, logits1, teacher, first, (devices, 2, STATS * BLOCK))
    every = lax.all_to_all(mine, VOCAB, 0, 0, tiled=True)
    grad0, loss0 = logit_grads(0, ids, e0, w0, mine, every)
    grad1, loss1 = logit_grads(1, ids, e1, w1, mine, after(grad0, every))
    pieces0, pieces1 = after(grad1, spread(grad0)), spread(grad1)
    give0, own_rows0, arrived0 = row_sums(pieces0)
    pieces1 = after(give0, pieces1)
    give1, own_rows1, arrived1 = row_sums(pieces1)
    loss = jnp.concatenate([loss0, loss1], axis=1)
    losses = [loss] + [shift(loss, "x", step) for step in (1, 2, 3)]
    head_grad = head_total(turned_hidden, (*pieces0, *pieces1))
    (head_grad, losses), arrived1 = lax.optimization_barrier(((head_grad, losses), arrived1))
    both = [
        own + part[0] + part[1] + part[2]
        for own, part in ((own_rows0, arrived0), (own_rows1, arrived1))
    ]
    both = jnp.concatenate(both, axis=1)
    both = lax.all_to_all(both, "z", 0, 0, tiled=True)
    both = both.sum(axis=0).astype(bf16)
    sum0, sum1 = both[:GROUP], both[GROUP:]
    keep = jnp.where(c == 0, sum0, sum1)
    got = shift(jnp.where(c == 0, sum1, sum0), "c", 1)
    low, high = jnp.where(c == 0, keep, got), jnp.where(c == 0, got, keep)
    hidden_grad = jnp.concatenate([low, high[:, BLOCK:]], axis=1)

    row = jnp.stack([part[0] for part in losses]).reshape(4, 2, 4, 2, GROUP)
    row = lax.dynamic_index_in_dim(row, x, 2, keepdims=False)
    row = jnp.take(row, (x - jnp.arange(4)) % 4, axis=0)
    loss_rows = row.transpose(2, 0, 1, 3).reshape(-1)
    return loss_rows, hidden_grad, head_grad


def solution(mesh):
    split = Mesh(mesh.devices.reshape(4, 4, 8, 2), ("x", "y", "z", "c"))
    in_specs = (P(None, "x"), P("x", VOCAB), P(None, "x"), P("x", VOCAB), P())
    out_specs = (P("x"), P(VOCAB, "x"), P("x", VOCAB))
    return jax.shard_map(body, mesh=split, in_specs=in_specs, out_specs=out_specs, check_vma=False)
```
